256 devices in a mesh: lat: 128 (over x, z, y), lev: 2 (over core).
Axes of the slice: x: 4, y: 4, z: 8, core: 2. Of those that a mesh axis runs over, the one named last changes fastest.
Arguments:
- grid: bfloat16 [768, 2, 48, 3088], P('lat', None, 'lev'), may hold values from -6 to 6
- point_counts: int32 [768], P('lat'), may hold values from 16 to 3088, as said below
- waves: int32 [768], replicated, may hold values from 0 to 767, each once
- legendre: bfloat16 [768, 768, 768], P('lat'), may hold values from -0.21875 to 0.21875
- weights: float32 [768], P('lat'), may hold values from 0.5 to 2
- stiffness: float32 [48], replicated, may hold values from 1e-06 to 0.0001
Outputs:
- grid_out: bfloat16 [768, 2, 48, 3088], P('lat', None, 'lev')
The draws below stay inside these ranges and needn't reach their ends.
Inputs may be any that keep to these rules, and one draw needn't show every extreme that they name: point_counts[j] is 4 j + 16 or 4 j + 20 (j counted from 0 at the pole), and the last pair has exactly 3088 points. `waves`: each wavenumber from 0 to 767 appears once.
All inputs are finite; a program needn't handle non-finite values.
Results may differ from the reference program's by a relative error of at most 0.015.
Values may be sent and summed in bfloat16 or wider, within the bound.
A program may use at most 128 MiB of HBM per device.

```python
import math
import jax
import jax.numpy as jnp
from jax import lax

M = 768
H = 768
NLON_MAX = 3088
F = 48


def draw_point_counts(key, part):
    latitude = jnp.arange(H, dtype=jnp.int32)
    extra = jax.random.randint(key, (H,), 0, 2).astype(jnp.int32)
    counts = 4 * latitude + 16 + 4 * extra
    return jnp.where(latitude == H - 1, 4 * H + 16, counts).astype(jnp.int32)


def level_of(rng, shape, shards, low, largest):
    gain, own = 1.0, jax.random.fold_in(rng, 6)
    for axis_at, blocks in shards:
        draws = jnp.exp(jax.random.uniform(jax.random.fold_in(own, axis_at), (blocks,), jnp.float32, low / len(shards), largest / len(shards)))
        gain = gain * jnp.repeat(draws, shape[axis_at] // blocks).reshape([-1 if axis == axis_at else 1 for axis in range(len(shape))])
    return gain


def scatter_about(stream_key, shape, deviation, limit, cuts=(), kind=jnp.bfloat16):
    gain = level_of(stream_key, shape, cuts, -0.22, 0.18) if cuts else 1.0
    result = jax.random.normal(stream_key, shape, jnp.float32) * deviation * gain
    return jnp.minimum(jnp.maximum(result, -limit), limit).astype(kind)


def setup_inputs(seed: int = 0) -> dict:
    splits = jax.random.split(jax.random.key(seed), 7)
    grid = scatter_about(splits[0], (H, 2, F, NLON_MAX), 1.0, 6.0, ((0, 128), (2, 2)))
    point_counts = draw_point_counts(jax.random.fold_in(splits[6], 71), 0)
    waves = jax.random.permutation(splits[2], M).astype(jnp.int32)
    legendre = scatter_about(splits[3], (M, H, M), H ** -0.5, 0.21875, ((0, 128),))
    weights = jnp.clip(jnp.exp(math.log(2.0) - 1.3862944 * jax.random.uniform(splits[4], (H,), jnp.float32) ** level_of(splits[4], (H,), ((0, 128),), -0.2, 0.2)), 0.5, 2.0)
    stiffness = jnp.clip(jnp.exp(jax.random.uniform(splits[5], (F,), jnp.float32, math.log(9.999999974752427e-07), math.log(0.0001))), 9.999999974752427e-07, 0.0001)
    return {"grid": grid, "point_counts": point_counts, "waves": waves, "legendre": legendre, "weights": weights, "stiffness": stiffness}


TWO_PI = 2.0 * math.pi
EXACT = lax.Precision.HIGHEST


def reference(grid, point_counts, waves, legendre, weights, stiffness):
    positions = jnp.arange(NLON_MAX, dtype=jnp.int32)
    degree_shift = jnp.arange(M, dtype=jnp.int32)
    parity = (1 - 2 * (degree_shift % 2)).astype(jnp.float32)

    def harmonics(count):
        phase = (positions[:, None] * waves[None, :]) % count
        angle = phase.astype(jnp.float32) * (TWO_PI / count.astype(jnp.float32))
        inside = (positions < count)[:, None]
        return jnp.where(inside, jnp.cos(angle), 0.0), jnp.where(inside, jnp.sin(angle), 0.0)

    def analyse(pieces):
        latitude, count, weight = pieces
        cosine, sine = harmonics(count)
        values = latitude.astype(jnp.float32)
        real = jnp.einsum("hfk,km->hfm", values, cosine, precision=EXACT)
        imag = -jnp.einsum("hfk,km->hfm", values, sine, precision=EXACT)
        factor = jnp.where(2 * waves < count, weight / count.astype(jnp.float32), 0.0)
        return jnp.stack([real * factor, imag * factor], axis=2).astype(jnp.bfloat16)

    coefficients = lax.map(analyse, (grid, point_counts, weights))
    by_slot = jnp.moveaxis(coefficients, 4, 0)

    def transform(pieces):
        block_data, basis, wavenumber = pieces
        basis_wide = basis.astype(jnp.float32)
        spectra = jnp.einsum("jhfr,jl->hfrl", block_data.astype(jnp.float32), basis_wide, precision=EXACT)
        combined = spectra[0] + parity * spectra[1]
        degrees = (wavenumber + degree_shift).astype(jnp.float32)
        inside_band = degree_shift < M - wavenumber
        factor = 1.0 / (1.0 + stiffness[:, None] * degrees[None, :] * (degrees[None, :] + 1.0))
        damping = jnp.where(inside_band[None, :], factor, 0.0)
        rounded = lax.optimization_barrier((combined * damping[:, None, :]).astype(jnp.bfloat16))
        scaled = rounded.astype(jnp.float32)
        operand = jnp.stack([scaled, scaled * parity], axis=0)
        returned = jnp.einsum("hfrl,jl->jhfr", operand, basis_wide, precision=EXACT)
        return returned.astype(jnp.bfloat16)

    synthesised = lax.map(transform, (by_slot, legendre, waves))
    fourier = jnp.moveaxis(synthesised, 0, 4)

    def synthesise(pieces):
        block_data, count = pieces
        cosine, sine = harmonics(count)
        factor = jnp.where(2 * waves < count, jnp.where(waves == 0, 1.0, 2.0), 0.0)
        real = block_data[:, :, 0, :].astype(jnp.float32) * factor
        imag = block_data[:, :, 1, :].astype(jnp.float32) * factor
        values = jnp.einsum("hfm,km->hfk", real, cosine, precision=EXACT) - jnp.einsum("hfm,km->hfk", imag, sine, precision=EXACT)
        return values.astype(jnp.bfloat16)

    return lax.map(synthesise, (fourier, point_counts))
```

```python
import functools
import math

import jax
import jax.numpy as jnp
from jax import lax
from jax.experimental import pallas as pl
from jax.experimental.pallas import tpu as pltpu
from jax.sharding import PartitionSpec as P

MESH = pl.DeviceIdType.MESH
F32 = jnp.float32
BF16 = jnp.bfloat16
LANES = 128
BLOCK = 256
FINE = 16
NT = (((1,), (1,)), ((), ()))


def cos_sin(steps, waves, count, inverse):
    product = steps * waves
    turns = jnp.floor(product * inverse + 0.5)
    half = (product - turns * count) * inverse * math.pi
    square = half * half
    sine = half
    term = 1.0
    series_s, series_c = 0.0, 0.0
    for power in range(5, -1, -1):
        series_s = series_s * square + (-1.0) ** power / math.factorial(2 * power + 1)
    for power in range(6, -1, -1):
        series_c = series_c * square + (-1.0) ** power / math.factorial(2 * power)
    sine = half * series_s
    return 1.0 - 2.0 * sine * sine, 2.0 * sine * series_c


def kernel(
    shape,
    grid_ref, counts_ref, weights_ref, waves_smem, waves_ref, stiffness_ref, legendre_ref,
    out_ref,
    tables, turn_c, turn_s, small_c, small_s, points, flat, spread, basis, ordered, perm, damping,
    spectra, scaled, operand, turned,
    send_a, recv_a, send_b, recv_b, basis_sem, send_sems, recv_sems,
):
    holders, pairs, fields, length, slots, width = shape
    chunks = 2
    lats = pairs // chunks
    blocks = -(-length // BLOCK)
    rows = 2 * fields
    parts = 2 * rows
    per_lat = slots * parts
    held = lats * per_lat
    pieces = -(-held // LANES)
    deep = send_a.shape[2]
    me = lax.axis_index("lat")
    lev = lax.axis_index("lev")

    barrier = pltpu.get_barrier_semaphore()

    def greet(k, carry):
        other = lax.rem(me + k, holders)
        pl.semaphore_signal(barrier, inc=1, device_id=(other, lev), device_id_type=MESH)
        return carry

    lax.fori_loop(1, holders, greet, 0)
    load_basis = pltpu.make_async_copy(legendre_ref, basis, basis_sem)
    load_basis.start()

    spread[...] = jnp.zeros_like(spread)
    flat[pl.ds(held, pieces * LANES - held), :] = jnp.zeros((pieces * LANES - held, LANES), F32)
    points[...] = jnp.zeros_like(points)

    def build_tables(i):
        count = jnp.full((1, width), counts_ref[i].astype(F32), F32)
        inverse = 1.0 / count
        waves = waves_ref[...].astype(F32)
        steps = lax.broadcasted_iota(jnp.int32, (FINE, width), 0).astype(F32)
        fine_c, fine_s = cos_sin(steps, waves, count, inverse)
        coarse_c, coarse_s = cos_sin(steps * FINE, waves, count, inverse)
        block_c, block_s = cos_sin(steps * BLOCK, waves, count, inverse)
        small_c[...] = coarse_c
        small_s[...] = coarse_s
        turn_c[i] = block_c
        turn_s[i] = block_s
        for g in range(BLOCK // FINE):
            c = small_c[g : g + 1, :]
            s = small_s[g : g + 1, :]
            tables[i, g * FINE : (g + 1) * FINE, :width] = (fine_c * c - fine_s * s).astype(BF16)
            tables[i, g * FINE : (g + 1) * FINE, width:] = (fine_s * c + fine_c * s).astype(BF16)

    def analyse(i, local):
        build_tables(i)
        total = counts_ref[i]
        for t in range(blocks):
            size = min(BLOCK, length - t * BLOCK)
            at = lax.broadcasted_iota(jnp.int32, (rows, size), 1) + t * BLOCK
            values = grid_ref[i, :, :, t * BLOCK : t * BLOCK + size].astype(F32)
            values = jnp.where(at < total, values.reshape(rows, size), 0.0)
            points[t * rows : (t + 1) * rows, :size] = values.astype(BF16)
        limit = total.astype(F32)
        scale = jnp.full((1, BLOCK), weights_ref[i], F32) / jnp.full((1, BLOCK), limit, F32)
        for n in range(width // BLOCK):
            lanes = slice(n * BLOCK, (n + 1) * BLOCK)
            by_c = jnp.dot(points[...], tables[i, :, lanes], preferred_element_type=F32)
            by_s = jnp.dot(
                points[...],
                tables[i, :, width + n * BLOCK : width + (n + 1) * BLOCK],
                preferred_element_type=F32,
            )
            real = by_c[:rows]
            imag = by_s[:rows]
            for t in range(1, blocks):
                c = turn_c[i, t : t + 1, lanes]
                s = turn_s[i, t : t + 1, lanes]
                zc = by_c[t * rows : (t + 1) * rows]
                zs = by_s[t * rows : (t + 1) * rows]
                real = real + (c * zc - s * zs)
                imag = imag + (s * zc + c * zs)
            inside = 2 * waves_ref[:, lanes] < total
            factor = jnp.where(inside, scale, 0.0)
            real = real * factor
            imag = -imag * factor
            for k in range(BLOCK // LANES):
                slot = n * (BLOCK // LANES) + k
                cut = slice(k * LANES, (k + 1) * LANES)
                for h in range(2):
                    base = local * per_lat + slot * parts + h * rows
                    if not isinstance(base, int):
                        base = pl.multiple_of(base, 8)
                    flat[pl.ds(base, fields), :] = real[h * fields : (h + 1) * fields, cut]
                    flat[pl.ds(base + fields, fields), :] = imag[h * fields : (h + 1) * fields, cut]

    def pack(target, chunk):
        for q in range(pieces):
            piece = flat[q * LANES : (q + 1) * LANES, :]
            spread[pl.ds(q, holders, stride=deep), :] = piece.T
        target[chunk] = spread[...].reshape(holders, deep, LANES).astype(BF16)

    def unpack(source, chunk):
        spread[...] = source[chunk].astype(F32).reshape(holders * deep, LANES)
        for q in range(pieces):
            flat[q * LANES : (q + 1) * LANES, :] = spread[pl.ds(q, holders, stride=deep), :].T

    def send(source, target, chunk, sem):
        def one(k, carry):
            other = lax.rem(me + k, holders)
            pltpu.make_async_remote_copy(
                src_ref=source.at[chunk, other],
                dst_ref=target.at[chunk, me],
                send_sem=send_sems.at[sem],
                recv_sem=recv_sems.at[sem],
                device_id=(other, lev),
                device_id_type=MESH,
            ).start()
            return carry

        lax.fori_loop(1, holders, one, 0)
        target[chunk, me] = source[chunk, me]

    def finish(ref, chunk, sem):
        most = ref.at[chunk, pl.ds(0, holders - 1)]
        pltpu.make_async_copy(most, most, sem).wait()

    for chunk in range(chunks):
        def step(local, carry):
            analyse(chunk * lats + local, local)
            return carry

        lax.fori_loop(0, lats, step, 0)
        pack(send_a, chunk)
        if chunk == 0:
            pl.semaphore_wait(barrier, holders - 1)
        send(send_a, recv_a, chunk, chunk)

    for i in range(pairs):
        place = lax.broadcasted_iota(jnp.int32, (holders, width), 0) * pairs + i
        at = lax.broadcasted_iota(jnp.int32, (holders, width), 1)
        perm[i * holders : (i + 1) * holders, :] = jnp.where(at == place, 1.0, 0.0).astype(BF16)
    load_basis.wait()

    levels = lax.broadcasted_iota(jnp.int32, (fields, stiffness_ref.shape[1]), 0) + lev * fields
    column = lax.broadcasted_iota(jnp.int32, (fields, stiffness_ref.shape[1]), 1)
    stiffness = jnp.sum(jnp.where(levels == column, stiffness_ref[...], 0.0), axis=1, keepdims=True)
    offsets = lax.broadcasted_iota(jnp.int32, (1, width), 1)
    parity = (1 - 2 * lax.rem(offsets, 2)).astype(F32)

    def prepare(s, carry):
        for m in range(width // BLOCK):
            part = slice(m * BLOCK, (m + 1) * BLOCK)
            ordered[s, part, :] = jnp.dot(
                perm[part, :], basis[s], preferred_element_type=F32
            ).astype(BF16)
        wave = waves_smem[me * slots + s]
        degrees = (offsets + wave).astype(F32)
        factor = 1.0 / (1.0 + stiffness * degrees * (degrees + 1.0))
        damping[s] = jnp.where(offsets < width - wave, factor, 0.0)
        return carry

    lax.fori_loop(0, slots, prepare, 0)

    half = lats * holders
    for chunk in range(chunks):
        finish(recv_a, chunk, recv_sems.at[chunk])
        unpack(recv_a, chunk)

        def forward(s, carry):
            pieces_of = [
                flat[pl.ds(pl.multiple_of(i * per_lat + s * parts, 8), parts), :].astype(BF16)
                for i in range(lats)
            ]
            part = jnp.dot(
                jnp.concatenate(pieces_of, axis=1),
                ordered[s, chunk * half : (chunk + 1) * half, :],
                preferred_element_type=F32,
            )
            if chunk == 0:
                spectra[s] = part
            else:
                part = part + spectra[s]
                combined = part[:rows] + parity * part[rows:]
                damp = jnp.concatenate([damping[s], damping[s]], axis=0)
                north = combined * damp
                scaled[s, :rows, :] = north.astype(BF16)
                scaled[s, rows:, :] = (north * parity).astype(BF16)
            return carry

        lax.fori_loop(0, slots, forward, 0)

    for chunk in range(chunks):
        def backward(s, carry):
            part = lax.dot_general(
                scaled[s],
                ordered[s, chunk * half : (chunk + 1) * half, :],
                NT,
                preferred_element_type=F32,
            )
            for i in range(lats):
                flat[pl.ds(pl.multiple_of(i * per_lat + s * parts, 8), parts), :] = part[
                    :, i * holders : (i + 1) * holders
                ]
            return carry

        lax.fori_loop(0, slots, backward, 0)
        pack(send_b, chunk)
        send(send_b, recv_b, chunk, chunks + chunk)

    def synthesise(i, local):
        total = counts_ref[i]
        inside = 2 * waves_ref[...] < total
        weight = jnp.where(inside, jnp.where(waves_ref[...] == 0, 1.0, 2.0), 0.0)
        for s in range(slots):
            lanes = slice(s * LANES, (s + 1) * LANES)
            for h in range(2):
                base = pl.multiple_of(local * per_lat + s * parts + h * rows, 8)
                operand[0, h * fields : (h + 1) * fields, lanes] = (
                    flat[pl.ds(base, fields), :] * weight[:, lanes]
                )
                operand[1, h * fields : (h + 1) * fields, lanes] = (
                    flat[pl.ds(base + fields, fields), :] * weight[:, lanes]
                )
        for n in range(width // BLOCK):
            lanes = slice(n * BLOCK, (n + 1) * BLOCK)
            real = operand[0, :, lanes]
            imag = operand[1, :, lanes]
            for t in range(blocks):
                c = turn_c[i, t : t + 1, lanes]
                s = turn_s[i, t : t + 1, lanes]
                turned[t * rows : (t + 1) * rows, lanes] = (real * c - imag * s).astype(BF16)
                turned[t * rows : (t + 1) * rows, width + n * BLOCK : width + (n + 1) * BLOCK] = (
                    -(real * s + imag * c)
                ).astype(BF16)
        result = lax.dot_general(turned[...], tables[i], NT, preferred_element_type=F32)
        for t in range(blocks):
            size = min(BLOCK, length - t * BLOCK)
            at = lax.broadcasted_iota(jnp.int32, (rows, size), 1) + t * BLOCK
            values = jnp.where(at < total, result[t * rows : (t + 1) * rows, :size], 0.0)
            out_ref[i, :, :, t * BLOCK : t * BLOCK + size] = values.reshape(2, fields, size).astype(BF16)

    for chunk in range(chunks):
        finish(recv_b, chunk, recv_sems.at[chunks + chunk])
        unpack(recv_b, chunk)

        def step_back(local, carry):
            synthesise(chunk * lats + local, local)
            return carry

        lax.fori_loop(0, lats, step_back, 0)

    for chunk in range(chunks):
        finish(send_a, chunk, send_sems.at[chunk])
        finish(send_b, chunk, send_sems.at[chunks + chunk])


def solution(mesh):
    holders = mesh.shape["lat"]

    def on_device(grid, point_counts, waves, legendre, weights, stiffness):
        pairs, _, fields, length = grid.shape
        slots, latitudes, width = legendre.shape
        blocks = -(-length // BLOCK)
        rows = 2 * fields
        held = (pairs // 2) * slots * 2 * rows
        pieces = -(-held // LANES)
        deep = -(-pieces // 16) * 16
        by_slot = waves.reshape(holders, slots).T.reshape(1, width)
        smem = pl.BlockSpec(memory_space=pltpu.SMEM)
        vmem = pl.BlockSpec(memory_space=pltpu.VMEM)
        message = pltpu.VMEM((2, holders, deep, LANES), BF16)
        return pl.pallas_call(
            functools.partial(kernel, (holders, pairs, fields, length, slots, width)),
            out_shape=jax.ShapeDtypeStruct(grid.shape, grid.dtype),
            in_specs=[vmem, smem, smem, smem, vmem, vmem, pl.BlockSpec(memory_space=pl.ANY)],
            out_specs=vmem,
            scratch_shapes=[
                pltpu.VMEM((pairs, BLOCK, 2 * width), BF16),
                pltpu.VMEM((pairs, FINE, width), F32),
                pltpu.VMEM((pairs, FINE, width), F32),
                pltpu.VMEM((FINE, width), F32),
                pltpu.VMEM((FINE, width), F32),
                pltpu.VMEM((blocks * rows, BLOCK), BF16),
                pltpu.VMEM((pieces * LANES, LANES), F32),
                pltpu.VMEM((holders * deep, LANES), F32),
                pltpu.VMEM((slots, latitudes, width), BF16),
                pltpu.VMEM((slots, latitudes, width), BF16),
                pltpu.VMEM((latitudes, width), BF16),
                pltpu.VMEM((slots, fields, width), F32),
                pltpu.VMEM((slots, 2 * rows, width), F32),
                pltpu.VMEM((slots, 2 * rows, width), BF16),
                pltpu.VMEM((2, rows, width), F32),
                pltpu.VMEM((blocks * rows, 2 * width), BF16),
                message,
                message,
                message,
                message,
                pltpu.SemaphoreType.DMA,
                pltpu.SemaphoreType.DMA((4,)),
                pltpu.SemaphoreType.DMA((4,)),
            ],
            compiler_params=pltpu.CompilerParams(
                collective_id=0, has_side_effects=True, vmem_limit_bytes=56 * 2**20
            ),
        )(grid, point_counts, weights, waves, by_slot, stiffness.reshape(1, -1), legendre)

    in_specs = (P("lat", None, "lev", None), P("lat"), P(), P("lat", None, None), P("lat"), P())
    out_specs = P("lat", None, "lev", None)
    return jax.shard_map(
        on_device, mesh=mesh, in_specs=in_specs, out_specs=out_specs, check_vma=False
    )
```

```python
import functools
import math

import jax
import jax.numpy as jnp
from jax import lax
from jax.experimental import pallas as pl
from jax.experimental.pallas import tpu as pltpu
from jax.sharding import PartitionSpec as P

MESH = pl.DeviceIdType.MESH
F32 = jnp.float32
BF16 = jnp.bfloat16
LANES = 128
BLOCK = 256
FINE = 16
VMEM_LIMIT = 60 * 2**20
NT = (((1,), (1,)), ((), ()))


def cos_sin(steps, waves, count, inverse):
    product = steps * waves
    turns = jnp.floor(product * inverse + 0.5)
    half = (product - turns * count) * inverse * math.pi
    square = half * half
    sine = half
    term = 1.0
    series_s, series_c = 0.0, 0.0
    for power in range(5, -1, -1):
        series_s = series_s * square + (-1.0) ** power / math.factorial(2 * power + 1)
    for power in range(6, -1, -1):
        series_c = series_c * square + (-1.0) ** power / math.factorial(2 * power)
    sine = half * series_s
    return 1.0 - 2.0 * sine * sine, 2.0 * sine * series_c


def kernel(
    shape,
    grid_ref, counts_ref, weights_ref, waves_smem, wave_row, stiffness_ref, legendre_ref,
    out_ref,
    waves_ref, tables, turn_c, turn_s, small_c, small_s, points, flat, spread, basis, ordered, perm, damping,
    spectra, scaled, operand, turned,
    send_a, recv_a, send_b, recv_b, basis_sem, send_sems, recv_sems,
):
    holders, pairs, fields, length, slots, width = shape
    chunks = 2
    lats = pairs // chunks
    blocks = -(-length // BLOCK)
    rows = 2 * fields
    parts = 2 * rows
    per_lat = slots * parts
    held = lats * per_lat
    pieces = -(-held // LANES)
    deep = 2 * send_a.shape[2]
    me = lax.axis_index("lat")
    lev = lax.axis_index("lev")

    barrier = pltpu.get_barrier_semaphore()

    def greet(k, carry):
        other = lax.rem(me + k, holders)
        pl.semaphore_signal(barrier, inc=1, device_id=(other, lev), device_id_type=MESH)
        return carry

    lax.fori_loop(1, holders, greet, 0)
    load_basis = pltpu.make_async_copy(legendre_ref, basis, basis_sem)
    load_basis.start()

    spread[...] = jnp.zeros_like(spread)
    flat[pl.ds(held, pieces * LANES - held), :] = jnp.zeros((pieces * LANES - held, LANES), F32)
    points[...] = jnp.zeros_like(points)

    for i in range(pairs):
        place = lax.broadcasted_iota(jnp.int32, (holders, width), 0) * pairs + i
        at = lax.broadcasted_iota(jnp.int32, (holders, width), 1)
        perm[i * holders : (i + 1) * holders, :] = jnp.where(at == place, 1.0, 0.0).astype(BF16)
    order = wave_row[...].reshape(1, width)
    first = lax.broadcasted_iota(jnp.int32, (16, width), 0) == 0
    digits = jnp.where(first, order // LANES, lax.rem(order, LANES))
    digits = lax.dot_general(
        digits.astype(F32).astype(BF16), perm[...], NT, preferred_element_type=F32
    )
    waves_ref[...] = digits[:1] * LANES + digits[1:2]

    def build_tables(i):
        count = jnp.full((1, width), counts_ref[i].astype(F32), F32)
        inverse = 1.0 / count
        waves = waves_ref[...]
        steps = lax.broadcasted_iota(jnp.int32, (FINE, width), 0).astype(F32)
        fine_c, fine_s = cos_sin(steps, waves, count, inverse)
        coarse_c, coarse_s = cos_sin(steps * FINE, waves, count, inverse)
        block_c, block_s = cos_sin(steps * BLOCK, waves, count, inverse)
        small_c[...] = coarse_c
        small_s[...] = coarse_s
        turn_c[i] = block_c
        turn_s[i] = block_s
        for g in range(BLOCK // FINE):
            c = small_c[g : g + 1, :]
            s = small_s[g : g + 1, :]
            tables[i, g * FINE : (g + 1) * FINE, :width] = (fine_c * c - fine_s * s).astype(BF16)
            tables[i, g * FINE : (g + 1) * FINE, width:] = (fine_s * c + fine_c * s).astype(BF16)

    def analyse(i, local):
        build_tables(i)
        total = counts_ref[i]
        for t in range(blocks):
            size = min(BLOCK, length - t * BLOCK)
            at = lax.broadcasted_iota(jnp.int32, (rows, size), 1) + t * BLOCK
            values = grid_ref[i, :, :, t * BLOCK : t * BLOCK + size].astype(F32)
            values = jnp.where(at < total, values.reshape(rows, size), 0.0)
            points[t * rows : (t + 1) * rows, :size] = values.astype(BF16)
        limit = total.astype(F32)
        scale = jnp.full((1, BLOCK), weights_ref[i], F32) / jnp.full((1, BLOCK), limit, F32)
        for n in range(width // BLOCK):
            lanes = slice(n * BLOCK, (n + 1) * BLOCK)
            by_c = jnp.dot(points[...], tables[i, :, lanes], preferred_element_type=F32)
            by_s = jnp.dot(
                points[...],
                tables[i, :, width + n * BLOCK : width + (n + 1) * BLOCK],
                preferred_element_type=F32,
            )
            real = by_c[:rows]
            imag = by_s[:rows]
            for t in range(1, blocks):
                c = turn_c[i, t : t + 1, lanes]
                s = turn_s[i, t : t + 1, lanes]
                zc = by_c[t * rows : (t + 1) * rows]
                zs = by_s[t * rows : (t + 1) * rows]
                real = real + (c * zc - s * zs)
                imag = imag + (s * zc + c * zs)
            inside = 2.0 * waves_ref[:, lanes] < limit
            factor = jnp.where(inside, scale, 0.0)
            real = real * factor
            imag = -imag * factor
            for k in range(BLOCK // LANES):
                slot = n * (BLOCK // LANES) + k
                cut = slice(k * LANES, (k + 1) * LANES)
                for h in range(2):
                    base = local * per_lat + slot * parts + h * rows
                    if not isinstance(base, int):
                        base = pl.multiple_of(base, 8)
                    flat[pl.ds(base, fields), :] = real[h * fields : (h + 1) * fields, cut]
                    flat[pl.ds(base + fields, fields), :] = imag[h * fields : (h + 1) * fields, cut]

    def pack(target, chunk):
        for q in range(pieces):
            piece = flat[q * LANES : (q + 1) * LANES, :]
            spread[pl.ds(q, holders, stride=deep), :] = piece.T
        pairs_of_rows = spread[...].reshape(holders * deep // 2, 2, LANES).astype(BF16)
        target[chunk] = pairs_of_rows.reshape(holders, deep // 2, 2, LANES)

    def unpack(source, chunk):
        spread[...] = source[chunk].astype(F32).reshape(holders * deep, LANES)
        for q in range(pieces):
            flat[q * LANES : (q + 1) * LANES, :] = spread[pl.ds(q, holders, stride=deep), :].T

    def send(source, target, chunk, sem):
        def one(k, carry):
            other = lax.rem(me + k, holders)
            pltpu.make_async_remote_copy(
                src_ref=source.at[chunk, other],
                dst_ref=target.at[chunk, me],
                send_sem=send_sems.at[sem],
                recv_sem=recv_sems.at[sem],
                device_id=(other, lev),
                device_id_type=MESH,
            ).start()
            return carry

        lax.fori_loop(1, holders, one, 0)
        target[chunk, me] = source[chunk, me]

    def finish(ref, chunk, sem):
        most = ref.at[chunk, pl.ds(0, holders - 1)]
        pltpu.make_async_copy(most, most, sem).wait()

    for chunk in range(chunks):
        def step(local, carry):
            analyse(chunk * lats + local, local)
            return carry

        lax.fori_loop(0, lats, step, 0)
        pack(send_a, chunk)
        if chunk == 0:
            pl.semaphore_wait(barrier, holders - 1)
        send(send_a, recv_a, chunk, chunk)

    load_basis.wait()

    levels = lax.broadcasted_iota(jnp.int32, (fields, stiffness_ref.shape[1]), 0) + lev * fields
    column = lax.broadcasted_iota(jnp.int32, (fields, stiffness_ref.shape[1]), 1)
    stiffness = jnp.sum(jnp.where(levels == column, stiffness_ref[...], 0.0), axis=1, keepdims=True)
    offsets = lax.broadcasted_iota(jnp.int32, (1, width), 1)
    parity = (1 - 2 * lax.rem(offsets, 2)).astype(F32)

    def prepare(s, carry):
        for m in range(width // BLOCK):
            part = slice(m * BLOCK, (m + 1) * BLOCK)
            ordered[s, part, :] = jnp.dot(
                perm[part, :], basis[s], preferred_element_type=F32
            ).astype(BF16)
        wave = waves_smem[me * slots + s]
        degrees = (offsets + wave).astype(F32)
        factor = 1.0 / (1.0 + stiffness * degrees * (degrees + 1.0))
        damping[s] = jnp.where(offsets < width - wave, factor, 0.0)
        return carry

    lax.fori_loop(0, slots, prepare, 0)

    half = lats * holders
    for chunk in range(chunks):
        finish(recv_a, chunk, recv_sems.at[chunk])
        unpack(recv_a, chunk)

        def forward(s, carry):
            pieces_of = [
                flat[pl.ds(pl.multiple_of(i * per_lat + s * parts, 8), parts), :].astype(BF16)
                for i in range(lats)
            ]
            part = jnp.dot(
                jnp.concatenate(pieces_of, axis=1),
                ordered[s, chunk * half : (chunk + 1) * half, :],
                preferred_element_type=F32,
            )
            if chunk == 0:
                spectra[s] = part
            else:
                part = part + spectra[s]
                combined = part[:rows] + parity * part[rows:]
                damp = jnp.concatenate([damping[s], damping[s]], axis=0)
                north = combined * damp
                scaled[s, :rows, :] = north.astype(BF16)
                scaled[s, rows:, :] = (north * parity).astype(BF16)
            return carry

        lax.fori_loop(0, slots, forward, 0)

    for chunk in range(chunks):
        def backward(s, carry):
            part = lax.dot_general(
                scaled[s],
                ordered[s, chunk * half : (chunk + 1) * half, :],
                NT,
                preferred_element_type=F32,
            )
            for i in range(lats):
                flat[pl.ds(pl.multiple_of(i * per_lat + s * parts, 8), parts), :] = part[
                    :, i * holders : (i + 1) * holders
                ]
            return carry

        lax.fori_loop(0, slots, backward, 0)
        pack(send_b, chunk)
        send(send_b, recv_b, chunk, chunks + chunk)

    def synthesise(i, local):
        total = counts_ref[i]
        inside = 2.0 * waves_ref[...] < total.astype(F32)
        weight = jnp.where(inside, jnp.where(waves_ref[...] == 0, 1.0, 2.0), 0.0)
        for s in range(slots):
            lanes = slice(s * LANES, (s + 1) * LANES)
            for h in range(2):
                base = pl.multiple_of(local * per_lat + s * parts + h * rows, 8)
                operand[0, h * fields : (h + 1) * fields, lanes] = (
                    flat[pl.ds(base, fields), :] * weight[:, lanes]
                )
                operand[1, h * fields : (h + 1) * fields, lanes] = (
                    flat[pl.ds(base + fields, fields), :] * weight[:, lanes]
                )
        for n in range(width // BLOCK):
            lanes = slice(n * BLOCK, (n + 1) * BLOCK)
            real = operand[0, :, lanes]
            imag = operand[1, :, lanes]
            for t in range(blocks):
                c = turn_c[i, t : t + 1, lanes]
                s = turn_s[i, t : t + 1, lanes]
                turned[t * rows : (t + 1) * rows, lanes] = (real * c - imag * s).astype(BF16)
                turned[t * rows : (t + 1) * rows, width + n * BLOCK : width + (n + 1) * BLOCK] = (
                    -(real * s + imag * c)
                ).astype(BF16)
        result = lax.dot_general(turned[...], tables[i], NT, preferred_element_type=F32)
        for t in range(blocks):
            size = min(BLOCK, length - t * BLOCK)
            at = lax.broadcasted_iota(jnp.int32, (rows, size), 1) + t * BLOCK
            values = jnp.where(at < total, result[t * rows : (t + 1) * rows, :size], 0.0)
            out_ref[i, :, :, t * BLOCK : t * BLOCK + size] = values.reshape(2, fields, size).astype(BF16)

    for chunk in range(chunks):
        finish(recv_b, chunk, recv_sems.at[chunks + chunk])
        unpack(recv_b, chunk)

        def step_back(local, carry):
            synthesise(chunk * lats + local, local)
            return carry

        lax.fori_loop(0, lats, step_back, 0)

    for chunk in range(chunks):
        finish(send_a, chunk, send_sems.at[chunk])
        finish(send_b, chunk, send_sems.at[chunks + chunk])


def write_out(source, target, sems):
    copies = [
        pltpu.make_async_copy(source.at[i], target.at[i], sems.at[i])
        for i in range(source.shape[0])
    ]
    for copy in copies:
        copy.start()
    for copy in copies:
        copy.wait()


def solution(mesh):
    holders = mesh.shape["lat"]

    def on_device(grid, point_counts, waves, legendre, weights, stiffness):
        pairs, _, fields, length = grid.shape
        slots, latitudes, width = legendre.shape
        blocks = -(-length // BLOCK)
        rows = 2 * fields
        held = (pairs // 2) * slots * 2 * rows
        pieces = -(-held // LANES)
        deep = -(-pieces // 2) * 2
        assert pairs == slots and holders * slots == width == latitudes
        smem = pl.BlockSpec(memory_space=pltpu.SMEM)
        vmem = pl.BlockSpec(memory_space=pltpu.VMEM)
        message = pltpu.VMEM((2, holders, deep // 2, 2, LANES), BF16)
        result = pl.pallas_call(
            functools.partial(kernel, (holders, pairs, fields, length, slots, width)),
            out_shape=pltpu.VMEM(grid.shape, grid.dtype),
            in_specs=[vmem, smem, smem, smem, vmem, vmem, pl.BlockSpec(memory_space=pl.ANY)],
            out_specs=vmem,
            scratch_shapes=[
                pltpu.VMEM((1, width), F32),
                pltpu.VMEM((pairs, BLOCK, 2 * width), BF16),
                pltpu.VMEM((pairs, FINE, width), F32),
                pltpu.VMEM((pairs, FINE, width), F32),
                pltpu.VMEM((FINE, width), F32),
                pltpu.VMEM((FINE, width), F32),
                pltpu.VMEM((blocks * rows, BLOCK), BF16),
                pltpu.VMEM((pieces * LANES, LANES), F32),
                pltpu.VMEM((holders * deep, LANES), F32),
                pltpu.VMEM((slots, latitudes, width), BF16),
                pltpu.VMEM((slots, latitudes, width), BF16),
                pltpu.VMEM((latitudes, width), BF16),
                pltpu.VMEM((slots, fields, width), F32),
                pltpu.VMEM((slots, 2 * rows, width), F32),
                pltpu.VMEM((slots, 2 * rows, width), BF16),
                pltpu.VMEM((2, rows, width), F32),
                pltpu.VMEM((blocks * rows, 2 * width), BF16),
                message,
                message,
                message,
                message,
                pltpu.SemaphoreType.DMA,
                pltpu.SemaphoreType.DMA((4,)),
                pltpu.SemaphoreType.DMA((4,)),
            ],
            compiler_params=pltpu.CompilerParams(
                collective_id=0, has_side_effects=True, vmem_limit_bytes=VMEM_LIMIT
            ),
        )(grid, point_counts, weights, waves, waves, stiffness.reshape(1, -1), legendre)
        anywhere = pl.BlockSpec(memory_space=pl.ANY)
        return pl.pallas_call(
            write_out,
            out_shape=jax.ShapeDtypeStruct(grid.shape, grid.dtype),
            in_specs=[vmem],
            out_specs=anywhere,
            scratch_shapes=[pltpu.SemaphoreType.DMA((pairs,))],
        )(pltpu.with_memory_space_constraint(result, pltpu.VMEM))

    in_specs = (P("lat", None, "lev", None), P("lat"), P(), P("lat", None, None), P("lat"), P())
    out_specs = P("lat", None, "lev", None)
    return jax.shard_map(
        on_device, mesh=mesh, in_specs=in_specs, out_specs=out_specs, check_vma=False
    )
```

```python
import functools
import math

import jax
import jax.numpy as jnp
from jax import lax
from jax.experimental import pallas as pl
from jax.experimental.pallas import tpu as pltpu
from jax.sharding import PartitionSpec as P

MESH = pl.DeviceIdType.MESH
F32 = jnp.float32
BF16 = jnp.bfloat16
LANES = 128
BLOCK = 256
FINE = 16
VMEM_LIMIT = 60 * 2**20
SPLIT = ((0, 8), (8, 16))
NT = (((1,), (1,)), ((), ()))


def cos_sin(steps, waves, count, inverse):
    product = steps * waves
    turns = jnp.floor(product * inverse + 0.5)
    half = (product - turns * count) * inverse * math.pi
    square = half * half
    sine = half
    term = 1.0
    series_s, series_c = 0.0, 0.0
    for power in range(5, -1, -1):
        series_s = series_s * square + (-1.0) ** power / math.factorial(2 * power + 1)
    for power in range(6, -1, -1):
        series_c = series_c * square + (-1.0) ** power / math.factorial(2 * power)
    sine = half * series_s
    return 1.0 - 2.0 * sine * sine, 2.0 * sine * series_c


def kernel(
    shape,
    grid_ref, counts_ref, weights_ref, waves_smem, wave_row, stiffness_ref, legendre_ref,
    out_ref,
    waves_ref, tables, turn_c, turn_s, small_c, small_s, flat, back, spread, basis, ordered, perm,
    damping, points, operand, turned, send_a, recv_a, send_b, recv_b, basis_sem, send_sems, recv_sems,
):
    holders, pairs, fields, length, slots, width = shape
    blocks = -(-length // BLOCK)
    me = lax.axis_index("lat")
    lev = lax.axis_index("lev")

    barrier = pltpu.get_barrier_semaphore()

    def greet(k, carry):
        other = lax.rem(me + k, holders)
        pl.semaphore_signal(barrier, inc=1, device_id=(other, lev), device_id_type=MESH)
        return carry

    lax.fori_loop(1, holders, greet, 0)
    load_basis = pltpu.make_async_copy(legendre_ref, basis, basis_sem)
    load_basis.start()

    for chunk, (_, count) in enumerate(SPLIT):
        held = pairs * slots * 4 * count
        rest = -held % (2 * LANES)
        if rest:
            flat[pl.ds(held, rest), :] = jnp.zeros((rest, LANES), F32)
            back[pl.ds(held, rest), :] = jnp.zeros((rest, LANES), F32)
        points[chunk][...] = jnp.zeros_like(points[chunk])

    for i in range(pairs):
        place = lax.broadcasted_iota(jnp.int32, (holders, width), 0) * pairs + i
        at = lax.broadcasted_iota(jnp.int32, (holders, width), 1)
        perm[i * holders : (i + 1) * holders, :] = jnp.where(at == place, 1.0, 0.0).astype(BF16)
    order = wave_row[...].reshape(1, width)
    first = lax.broadcasted_iota(jnp.int32, (16, width), 0) == 0
    digits = jnp.where(first, order // LANES, lax.rem(order, LANES))
    digits = lax.dot_general(
        digits.astype(F32).astype(BF16), perm[...], NT, preferred_element_type=F32
    )
    waves_ref[...] = digits[:1] * LANES + digits[1:2]

    def build_tables(i):
        count = jnp.full((1, width), counts_ref[i].astype(F32), F32)
        inverse = 1.0 / count
        waves = waves_ref[...]
        steps = lax.broadcasted_iota(jnp.int32, (FINE, width), 0).astype(F32)
        fine_c, fine_s = cos_sin(steps, waves, count, inverse)
        coarse_c, coarse_s = cos_sin(steps * FINE, waves, count, inverse)
        block_c, block_s = cos_sin(steps * BLOCK, waves, count, inverse)
        small_c[...] = coarse_c
        small_s[...] = coarse_s
        turn_c[i] = block_c
        turn_s[i] = block_s
        for g in range(BLOCK // FINE):
            c = small_c[g : g + 1, :]
            s = small_s[g : g + 1, :]
            tables[i, g * FINE : (g + 1) * FINE, :width] = (fine_c * c - fine_s * s).astype(BF16)
            tables[i, g * FINE : (g + 1) * FINE, width:] = (fine_s * c + fine_c * s).astype(BF16)

    def row_of(i, s, count, h, r):
        return pl.multiple_of(((i * slots + s) * 4 + h * 2 + r) * count, 8)

    def analyse(i, chunk):
        start, count = SPLIT[chunk]
        rows = 2 * count
        total = counts_ref[i]
        for t in range(blocks):
            size = min(BLOCK, length - t * BLOCK)
            at = lax.broadcasted_iota(jnp.int32, (rows, size), 1) + t * BLOCK
            values = grid_ref[i, :, start : start + count, t * BLOCK : t * BLOCK + size].astype(F32)
            values = jnp.where(at < total, values.reshape(rows, size), 0.0)
            points[chunk][t * rows : (t + 1) * rows, :size] = values.astype(BF16)
        limit = total.astype(F32)
        scale = jnp.full((1, BLOCK), weights_ref[i], F32) / jnp.full((1, BLOCK), limit, F32)
        for n in range(width // BLOCK):
            lanes = slice(n * BLOCK, (n + 1) * BLOCK)
            by_c = jnp.dot(points[chunk][...], tables[i, :, lanes], preferred_element_type=F32)
            by_s = jnp.dot(
                points[chunk][...],
                tables[i, :, width + n * BLOCK : width + (n + 1) * BLOCK],
                preferred_element_type=F32,
            )
            real = by_c[:rows]
            imag = by_s[:rows]
            for t in range(1, blocks):
                c = turn_c[i, t : t + 1, lanes]
                s = turn_s[i, t : t + 1, lanes]
                zc = by_c[t * rows : (t + 1) * rows]
                zs = by_s[t * rows : (t + 1) * rows]
                real = real + (c * zc - s * zs)
                imag = imag + (s * zc + c * zs)
            inside = 2.0 * waves_ref[:, lanes] < limit
            factor = jnp.where(inside, scale, 0.0)
            real = real * factor
            imag = -imag * factor
            for k in range(BLOCK // LANES):
                slot = n * (BLOCK // LANES) + k
                cut = slice(k * LANES, (k + 1) * LANES)
                for h in range(2):
                    part = slice(h * count, (h + 1) * count)
                    flat[pl.ds(row_of(i, slot, count, h, 0), count), :] = real[part, cut]
                    flat[pl.ds(row_of(i, slot, count, h, 1), count), :] = imag[part, cut]

    def pack(source, target):
        deep = 2 * target.shape[1]
        for q in range(deep):
            piece = source[q * LANES : (q + 1) * LANES, :]
            spread[pl.ds(q, holders, stride=deep), :] = piece.T
        twos = spread[pl.ds(0, holders * deep), :].reshape(holders * deep // 2, 2, LANES).astype(BF16)
        target[...] = twos.reshape(holders, deep // 2, 2, LANES)

    def unpack(source):
        deep = 2 * source.shape[1]
        spread[pl.ds(0, holders * deep), :] = source[...].astype(F32).reshape(holders * deep, LANES)
        for q in range(deep):
            flat[q * LANES : (q + 1) * LANES, :] = spread[pl.ds(q, holders, stride=deep), :].T

    def send(source, target, sem):
        def one(k, carry):
            other = lax.rem(me + k, holders)
            pltpu.make_async_remote_copy(
                src_ref=source.at[other],
                dst_ref=target.at[me],
                send_sem=send_sems.at[sem],
                recv_sem=recv_sems.at[sem],
                device_id=(other, lev),
                device_id_type=MESH,
            ).start()
            return carry

        lax.fori_loop(1, holders, one, 0)
        target[me] = source[me]

    def finish(ref, sem):
        most = ref.at[pl.ds(0, holders - 1)]
        pltpu.make_async_copy(most, most, sem).wait()

    chunks = len(SPLIT)
    for chunk in range(chunks):
        def step(i, carry):
            if chunk == 0:
                build_tables(i)
            analyse(i, chunk)
            return carry

        lax.fori_loop(0, pairs, step, 0)
        pack(flat, send_a[chunk])
        if chunk == 0:
            pl.semaphore_wait(barrier, holders - 1)
        send(send_a[chunk], recv_a[chunk], chunk)

    load_basis.wait()
    levels = lax.broadcasted_iota(jnp.int32, (fields, stiffness_ref.shape[1]), 0) + lev * fields
    column = lax.broadcasted_iota(jnp.int32, (fields, stiffness_ref.shape[1]), 1)
    stiffness = jnp.sum(jnp.where(levels == column, stiffness_ref[...], 0.0), axis=1, keepdims=True)
    offsets = lax.broadcasted_iota(jnp.int32, (1, width), 1)
    parity = (1 - 2 * lax.rem(offsets, 2)).astype(F32)

    def prepare(s, carry):
        for m in range(width // BLOCK):
            part = slice(m * BLOCK, (m + 1) * BLOCK)
            ordered[s, part, :] = jnp.dot(
                perm[part, :], basis[s], preferred_element_type=F32
            ).astype(BF16)
        wave = waves_smem[me * slots + s]
        degrees = (offsets + wave).astype(F32)
        factor = 1.0 / (1.0 + stiffness * degrees * (degrees + 1.0))
        damping[s] = jnp.where(offsets < width - wave, factor, 0.0)
        return carry

    lax.fori_loop(0, slots, prepare, 0)

    for chunk, (start, count) in enumerate(SPLIT):
        finish(recv_a[chunk], recv_sems.at[chunk])
        unpack(recv_a[chunk])

        def transform(s, carry):
            parts = [flat[pl.ds(row_of(i, s, count, 0, 0), 4 * count), :].astype(BF16) for i in range(pairs)]
            spectra = jnp.dot(
                jnp.concatenate(parts, axis=1), ordered[s], preferred_element_type=F32
            )
            combined = spectra[: 2 * count] + parity * spectra[2 * count :]
            damp = damping[s, start : start + count, :]
            scaled = combined * jnp.concatenate([damp, damp], axis=0)
            both = jnp.concatenate([scaled.astype(BF16), (scaled * parity).astype(BF16)], axis=0)
            result = lax.dot_general(both, ordered[s], NT, preferred_element_type=F32)
            for i in range(pairs):
                back[pl.ds(row_of(i, s, count, 0, 0), 4 * count), :] = result[
                    :, i * holders : (i + 1) * holders
                ]
            return carry

        lax.fori_loop(0, slots, transform, 0)
        pack(back, send_b[chunk])
        send(send_b[chunk], recv_b[chunk], chunks + chunk)

    def synthesise(i, chunk):
        start, count = SPLIT[chunk]
        rows = 2 * count
        total = counts_ref[i]
        inside = 2.0 * waves_ref[...] < total.astype(F32)
        weight = jnp.where(inside, jnp.where(waves_ref[...] == 0, 1.0, 2.0), 0.0)
        for s in range(slots):
            lanes = slice(s * LANES, (s + 1) * LANES)
            for h in range(2):
                part = slice(h * count, (h + 1) * count)
                for r in range(2):
                    operand[r, part, lanes] = (
                        flat[pl.ds(row_of(i, s, count, h, r), count), :] * weight[:, lanes]
                    )
        for n in range(width // BLOCK):
            lanes = slice(n * BLOCK, (n + 1) * BLOCK)
            real = operand[0, :rows, lanes]
            imag = operand[1, :rows, lanes]
            for t in range(blocks):
                c = turn_c[i, t : t + 1, lanes]
                s = turn_s[i, t : t + 1, lanes]
                turned[t * rows : (t + 1) * rows, lanes] = (real * c - imag * s).astype(BF16)
                turned[t * rows : (t + 1) * rows, width + n * BLOCK : width + (n + 1) * BLOCK] = (
                    -(real * s + imag * c)
                ).astype(BF16)
        result = lax.dot_general(
            turned[: blocks * rows, :], tables[i], NT, preferred_element_type=F32
        )
        for t in range(blocks):
            size = min(BLOCK, length - t * BLOCK)
            at = lax.broadcasted_iota(jnp.int32, (rows, size), 1) + t * BLOCK
            values = jnp.where(at < total, result[t * rows : (t + 1) * rows, :size], 0.0)
            out_ref[i, :, start : start + count, t * BLOCK : t * BLOCK + size] = values.reshape(
                2, count, size
            ).astype(BF16)

    for chunk in range(chunks):
        finish(recv_b[chunk], recv_sems.at[chunks + chunk])
        unpack(recv_b[chunk])

        def step_back(i, carry):
            synthesise(i, chunk)
            return carry

        lax.fori_loop(0, pairs, step_back, 0)

    for chunk in range(chunks):
        finish(send_a[chunk], send_sems.at[chunk])
        finish(send_b[chunk], send_sems.at[chunks + chunk])


def write_out(source, target, sems):
    copies = [
        pltpu.make_async_copy(source.at[i], target.at[i], sems.at[i])
        for i in range(source.shape[0])
    ]
    for copy in copies:
        copy.start()
    for copy in copies:
        copy.wait()


def solution(mesh):
    holders = mesh.shape["lat"]

    def on_device(grid, point_counts, waves, legendre, weights, stiffness):
        pairs, _, fields, length = grid.shape
        slots, latitudes, width = legendre.shape
        blocks = -(-length // BLOCK)
        most = max(count for _, count in SPLIT)
        deep = [-(-pairs * slots * 4 * count // (2 * LANES)) for _, count in SPLIT]
        messages = [pltpu.VMEM((holders, pieces, 2, LANES), BF16) for pieces in deep]
        assert pairs == slots and holders * slots == width == latitudes
        assert sum(count for _, count in SPLIT) == fields
        smem = pl.BlockSpec(memory_space=pltpu.SMEM)
        vmem = pl.BlockSpec(memory_space=pltpu.VMEM)
        result = pl.pallas_call(
            functools.partial(kernel, (holders, pairs, fields, length, slots, width)),
            out_shape=pltpu.VMEM(grid.shape, grid.dtype),
            in_specs=[vmem, smem, smem, smem, vmem, vmem, pl.BlockSpec(memory_space=pl.ANY)],
            out_specs=vmem,
            scratch_shapes=[
                pltpu.VMEM((1, width), F32),
                pltpu.VMEM((pairs, BLOCK, 2 * width), BF16),
                pltpu.VMEM((pairs, FINE, width), F32),
                pltpu.VMEM((pairs, FINE, width), F32),
                pltpu.VMEM((FINE, width), F32),
                pltpu.VMEM((FINE, width), F32),
                pltpu.VMEM((2 * max(deep) * LANES, LANES), F32),
                pltpu.VMEM((2 * max(deep) * LANES, LANES), F32),
                pltpu.VMEM((2 * max(deep) * holders, LANES), F32),
                pltpu.VMEM((slots, latitudes, width), BF16),
                pltpu.VMEM((slots, latitudes, width), BF16),
                pltpu.VMEM((latitudes, width), BF16),
                pltpu.VMEM((slots, fields, width), F32),
                [pltpu.VMEM((blocks * 2 * count, BLOCK), BF16) for _, count in SPLIT],
                pltpu.VMEM((2, 2 * most, width), F32),
                pltpu.VMEM((blocks * 2 * most, 2 * width), BF16),
                messages,
                messages,
                messages,
                messages,
                pltpu.SemaphoreType.DMA,
                pltpu.SemaphoreType.DMA((2 * len(SPLIT),)),
                pltpu.SemaphoreType.DMA((2 * len(SPLIT),)),
            ],
            compiler_params=pltpu.CompilerParams(
                collective_id=0, has_side_effects=True, vmem_limit_bytes=VMEM_LIMIT
            ),
        )(grid, point_counts, weights, waves, waves, stiffness.reshape(1, -1), legendre)
        anywhere = pl.BlockSpec(memory_space=pl.ANY)
        return pl.pallas_call(
            write_out,
            out_shape=jax.ShapeDtypeStruct(grid.shape, grid.dtype),
            in_specs=[vmem],
            out_specs=anywhere,
            scratch_shapes=[pltpu.SemaphoreType.DMA((pairs,))],
        )(pltpu.with_memory_space_constraint(result, pltpu.VMEM))

    in_specs = (P("lat", None, "lev", None), P("lat"), P(), P("lat", None, None), P("lat"), P())
    out_specs = P("lat", None, "lev", None)
    return jax.shard_map(
        on_device, mesh=mesh, in_specs=in_specs, out_specs=out_specs, check_vma=False
    )
```

```python
import functools
import math

import jax
import jax.numpy as jnp
from jax import lax
from jax.experimental import pallas as pl
from jax.experimental.pallas import tpu as pltpu
from jax.sharding import PartitionSpec as P

MESH = pl.DeviceIdType.MESH
F32 = jnp.float32
BF16 = jnp.bfloat16
LANES = 128
BLOCK = 256
FINE = 16
VMEM_LIMIT = 60 * 2**20
SPLIT = ((0, 8), (8, 16))
OUTWARD = (((0, 6),), ((0, 6),))
HOMEWARD = (((0, 6),), ((0, 2), (2, 2), (4, 2)))
NT = (((1,), (1,)), ((), ()))


def cos_sin(steps, waves, count, inverse):
    product = steps * waves
    turns = jnp.floor(product * inverse + 0.5)
    half = (product - turns * count) * inverse * math.pi
    square = half * half
    sine = half
    term = 1.0
    series_s, series_c = 0.0, 0.0
    for power in range(5, -1, -1):
        series_s = series_s * square + (-1.0) ** power / math.factorial(2 * power + 1)
    for power in range(6, -1, -1):
        series_c = series_c * square + (-1.0) ** power / math.factorial(2 * power)
    sine = half * series_s
    return 1.0 - 2.0 * sine * sine, 2.0 * sine * series_c


def kernel(
    shape,
    grid_ref, counts_ref, weights_ref, waves_smem, wave_row, stiffness_ref, legendre_ref,
    out_ref,
    waves_ref, tables, turn_c, turn_s, small_c, small_s, flat, back, spread, basis, ordered, perm,
    scaled,
    damping, points, operand, turned, send_a, recv_a, send_b, recv_b, basis_sem, send_sems, recv_sems,
):
    holders, pairs, fields, length, slots, width = shape
    blocks = -(-length // BLOCK)
    me = lax.axis_index("lat")
    lev = lax.axis_index("lev")

    barrier = pltpu.get_barrier_semaphore()

    def greet(k, carry):
        other = lax.rem(me + k, holders)
        pl.semaphore_signal(barrier, inc=1, device_id=(other, lev), device_id_type=MESH)
        return carry

    lax.fori_loop(1, holders, greet, 0)
    load_basis = pltpu.make_async_copy(legendre_ref, basis, basis_sem)
    load_basis.start()

    spread[...] = jnp.zeros_like(spread)
    for ref in points:
        ref[...] = jnp.zeros_like(ref)

    for i in range(pairs):
        place = lax.broadcasted_iota(jnp.int32, (holders, width), 0) * pairs + i
        at = lax.broadcasted_iota(jnp.int32, (holders, width), 1)
        perm[i * holders : (i + 1) * holders, :] = jnp.where(at == place, 1.0, 0.0).astype(BF16)
    order = wave_row[...].reshape(1, width)
    first = lax.broadcasted_iota(jnp.int32, (16, width), 0) == 0
    digits = jnp.where(first, order // LANES, lax.rem(order, LANES))
    digits = lax.dot_general(
        digits.astype(F32).astype(BF16), perm[...], NT, preferred_element_type=F32
    )
    waves_ref[...] = digits[:1] * LANES + digits[1:2]

    def build_tables(i):
        count = jnp.full((1, width), counts_ref[i].astype(F32), F32)
        inverse = 1.0 / count
        waves = waves_ref[...]
        steps = lax.broadcasted_iota(jnp.int32, (FINE, width), 0).astype(F32)
        fine_c, fine_s = cos_sin(steps, waves, count, inverse)
        coarse_c, coarse_s = cos_sin(steps * FINE, waves, count, inverse)
        block_c, block_s = cos_sin(steps * BLOCK, waves, count, inverse)
        small_c[...] = coarse_c
        small_s[...] = coarse_s
        turn_c[i] = block_c
        turn_s[i] = block_s
        for g in range(BLOCK // FINE):
            c = small_c[g : g + 1, :]
            s = small_s[g : g + 1, :]
            tables[i, g * FINE : (g + 1) * FINE, :width] = (fine_c * c - fine_s * s).astype(BF16)
            tables[i, g * FINE : (g + 1) * FINE, width:] = (fine_s * c + fine_c * s).astype(BF16)

    def row_of(i, s, count, h, r):
        return pl.multiple_of(((i * slots + s) * 4 + h * 2 + r) * count, 8)

    def analyse(i, chunk):
        start, count = SPLIT[chunk]
        rows = 2 * count
        total = counts_ref[i]
        for t in range(blocks):
            size = min(BLOCK, length - t * BLOCK)
            at = lax.broadcasted_iota(jnp.int32, (rows, size), 1) + t * BLOCK
            values = grid_ref[i, :, start : start + count, t * BLOCK : t * BLOCK + size].astype(F32)
            values = jnp.where(at < total, values.reshape(rows, size), 0.0)
            points[chunk][t * rows : (t + 1) * rows, :size] = values.astype(BF16)
        limit = total.astype(F32)
        scale = jnp.full((1, BLOCK), weights_ref[i], F32) / jnp.full((1, BLOCK), limit, F32)
        for n in range(width // BLOCK):
            lanes = slice(n * BLOCK, (n + 1) * BLOCK)
            by_c = jnp.dot(points[chunk][...], tables[i, :, lanes], preferred_element_type=F32)
            by_s = jnp.dot(
                points[chunk][...],
                tables[i, :, width + n * BLOCK : width + (n + 1) * BLOCK],
                preferred_element_type=F32,
            )
            real = by_c[:rows]
            imag = by_s[:rows]
            for t in range(1, blocks):
                c = turn_c[i, t : t + 1, lanes]
                s = turn_s[i, t : t + 1, lanes]
                zc = by_c[t * rows : (t + 1) * rows]
                zs = by_s[t * rows : (t + 1) * rows]
                real = real + (c * zc - s * zs)
                imag = imag + (s * zc + c * zs)
            inside = 2.0 * waves_ref[:, lanes] < limit
            factor = jnp.where(inside, scale, 0.0)
            real = real * factor
            imag = -imag * factor
            for k in range(BLOCK // LANES):
                slot = n * (BLOCK // LANES) + k
                cut = slice(k * LANES, (k + 1) * LANES)
                for h in range(2):
                    part = slice(h * count, (h + 1) * count)
                    flat[pl.ds(row_of(i, slot, count, h, 0), count), :] = real[part, cut]
                    flat[pl.ds(row_of(i, slot, count, h, 1), count), :] = imag[part, cut]

    def cut_of(chunk, first, number):
        size = slots * 4 * SPLIT[chunk][1]
        return first * size, number * size // LANES

    def pack(source, target, cut):
        deep = 2 * target.shape[1]
        base, pieces = cut
        for q in range(pieces):
            piece = source[base + q * LANES : base + (q + 1) * LANES, :]
            spread[pl.ds(q, holders, stride=deep), :] = piece.T
        twos = spread[pl.ds(0, holders * deep), :].reshape(holders * deep // 2, 2, LANES).astype(BF16)
        target[...] = twos.reshape(holders, deep // 2, 2, LANES)

    def unpack(source, cut):
        deep = 2 * source.shape[1]
        base, pieces = cut
        spread[pl.ds(0, holders * deep), :] = source[...].astype(F32).reshape(holders * deep, LANES)
        for q in range(pieces):
            flat[base + q * LANES : base + (q + 1) * LANES, :] = spread[
                pl.ds(q, holders, stride=deep), :
            ].T

    def send(source, target, sem):
        def one(k, carry):
            other = lax.rem(me + k, holders)
            pltpu.make_async_remote_copy(
                src_ref=source.at[other],
                dst_ref=target.at[me],
                send_sem=send_sems.at[sem],
                recv_sem=recv_sems.at[sem],
                device_id=(other, lev),
                device_id_type=MESH,
            ).start()
            return carry

        lax.fori_loop(1, holders, one, 0)
        target[me] = source[me]

    def finish(ref, sem):
        most = ref.at[pl.ds(0, holders - 1)]
        pltpu.make_async_copy(most, most, sem).wait()

    outward = [(chunk, cut) for chunk, cuts in enumerate(OUTWARD) for cut in cuts]
    homeward = [(chunk, cut) for chunk, cuts in enumerate(HOMEWARD) for cut in cuts]
    for index, (chunk, (first_lat, number)) in enumerate(outward):
        def step(i, carry):
            if chunk == 0:
                build_tables(i)
            analyse(i, chunk)
            return carry

        lax.fori_loop(first_lat, first_lat + number, step, 0)
        pack(flat, send_a[index], cut_of(chunk, first_lat, number))
        if index == 0:
            pl.semaphore_wait(barrier, holders - 1)
        send(send_a[index], recv_a[index], index)

    load_basis.wait()
    levels = lax.broadcasted_iota(jnp.int32, (fields, stiffness_ref.shape[1]), 0) + lev * fields
    column = lax.broadcasted_iota(jnp.int32, (fields, stiffness_ref.shape[1]), 1)
    stiffness = jnp.sum(jnp.where(levels == column, stiffness_ref[...], 0.0), axis=1, keepdims=True)
    offsets = lax.broadcasted_iota(jnp.int32, (1, width), 1)
    parity = (1 - 2 * lax.rem(offsets, 2)).astype(F32)

    def prepare(s, carry):
        for m in range(width // BLOCK):
            part = slice(m * BLOCK, (m + 1) * BLOCK)
            ordered[s, part, :] = jnp.dot(
                perm[part, :], basis[s], preferred_element_type=F32
            ).astype(BF16)
        wave = waves_smem[me * slots + s]
        degrees = (offsets + wave).astype(F32)
        factor = 1.0 / (1.0 + stiffness * degrees * (degrees + 1.0))
        damping[s] = jnp.where(offsets < width - wave, factor, 0.0)
        return carry

    lax.fori_loop(0, slots, prepare, 0)

    for chunk, (start, count) in enumerate(SPLIT):
        for index, (of, cut) in enumerate(outward):
            if of == chunk:
                finish(recv_a[index], recv_sems.at[index])
                unpack(recv_a[index], cut_of(chunk, *cut))

        def project(s, carry):
            parts = [flat[pl.ds(row_of(i, s, count, 0, 0), 4 * count), :].astype(BF16) for i in range(pairs)]
            spectra = jnp.dot(
                jnp.concatenate(parts, axis=1), ordered[s], preferred_element_type=F32
            )
            combined = spectra[: 2 * count] + parity * spectra[2 * count :]
            damp = damping[s, start : start + count, :]
            north = combined * jnp.concatenate([damp, damp], axis=0)
            scaled[s, : 2 * count, :] = north.astype(BF16)
            scaled[s, 2 * count : 4 * count, :] = (north * parity).astype(BF16)
            return carry

        lax.fori_loop(0, slots, project, 0)
        for index, (of, (first_lat, number)) in enumerate(homeward):
            if of != chunk:
                continue

            def restore(s, carry):
                result = lax.dot_general(
                    scaled[s, : 4 * count, :],
                    ordered[s, first_lat * holders : (first_lat + number) * holders, :],
                    NT,
                    preferred_element_type=F32,
                )
                for i in range(number):
                    back[pl.ds(row_of(first_lat + i, s, count, 0, 0), 4 * count), :] = result[
                        :, i * holders : (i + 1) * holders
                    ]
                return carry

            lax.fori_loop(0, slots, restore, 0)
            pack(back, send_b[index], cut_of(chunk, first_lat, number))
            send(send_b[index], recv_b[index], len(outward) + index)

    def synthesise(i, chunk):
        start, count = SPLIT[chunk]
        rows = 2 * count
        total = counts_ref[i]
        inside = 2.0 * waves_ref[...] < total.astype(F32)
        weight = jnp.where(inside, jnp.where(waves_ref[...] == 0, 1.0, 2.0), 0.0)
        for s in range(slots):
            lanes = slice(s * LANES, (s + 1) * LANES)
            for h in range(2):
                part = slice(h * count, (h + 1) * count)
                for r in range(2):
                    operand[r, part, lanes] = (
                        flat[pl.ds(row_of(i, s, count, h, r), count), :] * weight[:, lanes]
                    )
        for n in range(width // BLOCK):
            lanes = slice(n * BLOCK, (n + 1) * BLOCK)
            real = operand[0, :rows, lanes]
            imag = operand[1, :rows, lanes]
            for t in range(blocks):
                c = turn_c[i, t : t + 1, lanes]
                s = turn_s[i, t : t + 1, lanes]
                turned[t * rows : (t + 1) * rows, lanes] = (real * c - imag * s).astype(BF16)
                turned[t * rows : (t + 1) * rows, width + n * BLOCK : width + (n + 1) * BLOCK] = (
                    -(real * s + imag * c)
                ).astype(BF16)
        result = lax.dot_general(
            turned[: blocks * rows, :], tables[i], NT, preferred_element_type=F32
        )
        for t in range(blocks):
            size = min(BLOCK, length - t * BLOCK)
            at = lax.broadcasted_iota(jnp.int32, (rows, size), 1) + t * BLOCK
            values = jnp.where(at < total, result[t * rows : (t + 1) * rows, :size], 0.0)
            out_ref[i, :, start : start + count, t * BLOCK : t * BLOCK + size] = values.reshape(
                2, count, size
            ).astype(BF16)

    for index, (chunk, (first_lat, number)) in enumerate(homeward):
        finish(recv_b[index], recv_sems.at[len(outward) + index])
        unpack(recv_b[index], cut_of(chunk, first_lat, number))

        def step_back(i, carry):
            synthesise(i, chunk)
            return carry

        lax.fori_loop(first_lat, first_lat + number, step_back, 0)

    for index in range(len(outward)):
        finish(send_a[index], send_sems.at[index])
    for index in range(len(homeward)):
        finish(send_b[index], send_sems.at[len(outward) + index])


def write_out(source, target, sems):
    copies = [
        pltpu.make_async_copy(source.at[i], target.at[i], sems.at[i])
        for i in range(source.shape[0])
    ]
    for copy in copies:
        copy.start()
    for copy in copies:
        copy.wait()


def solution(mesh):
    holders = mesh.shape["lat"]

    def on_device(grid, point_counts, waves, legendre, weights, stiffness):
        pairs, _, fields, length = grid.shape
        slots, latitudes, width = legendre.shape
        blocks = -(-length // BLOCK)
        most = max(count for _, count in SPLIT)
        def messages(plan):
            sizes = [
                number * slots * 4 * SPLIT[chunk][1]
                for chunk, cuts in enumerate(plan)
                for _, number in cuts
            ]
            assert all(size % LANES == 0 for size in sizes)
            return [pltpu.VMEM((holders, -(-size // (2 * LANES)), 2, LANES), BF16) for size in sizes]

        outward, homeward = messages(OUTWARD), messages(HOMEWARD)
        deep = 2 * max(message.shape[1] for message in outward + homeward)
        held = pairs * slots * 4 * most
        assert pairs == slots and holders * slots == width == latitudes
        assert sum(count for _, count in SPLIT) == fields
        smem = pl.BlockSpec(memory_space=pltpu.SMEM)
        vmem = pl.BlockSpec(memory_space=pltpu.VMEM)
        result = pl.pallas_call(
            functools.partial(kernel, (holders, pairs, fields, length, slots, width)),
            out_shape=pltpu.VMEM(grid.shape, grid.dtype),
            in_specs=[vmem, smem, smem, smem, vmem, vmem, pl.BlockSpec(memory_space=pl.ANY)],
            out_specs=vmem,
            scratch_shapes=[
                pltpu.VMEM((1, width), F32),
                pltpu.VMEM((pairs, BLOCK, 2 * width), BF16),
                pltpu.VMEM((pairs, FINE, width), F32),
                pltpu.VMEM((pairs, FINE, width), F32),
                pltpu.VMEM((FINE, width), F32),
                pltpu.VMEM((FINE, width), F32),
                pltpu.VMEM((held, LANES), F32),
                pltpu.VMEM((held, LANES), F32),
                pltpu.VMEM((deep * holders, LANES), F32),
                pltpu.VMEM((slots, latitudes, width), BF16),
                pltpu.VMEM((slots, latitudes, width), BF16),
                pltpu.VMEM((latitudes, width), BF16),
                pltpu.VMEM((slots, 4 * most, width), BF16),
                pltpu.VMEM((slots, fields, width), F32),
                [pltpu.VMEM((blocks * 2 * count, BLOCK), BF16) for _, count in SPLIT],
                pltpu.VMEM((2, 2 * most, width), F32),
                pltpu.VMEM((blocks * 2 * most, 2 * width), BF16),
                outward,
                outward,
                homeward,
                homeward,
                pltpu.SemaphoreType.DMA,
                pltpu.SemaphoreType.DMA((len(outward) + len(homeward),)),
                pltpu.SemaphoreType.DMA((len(outward) + len(homeward),)),
            ],
            compiler_params=pltpu.CompilerParams(
                collective_id=0, has_side_effects=True, vmem_limit_bytes=VMEM_LIMIT
            ),
        )(grid, point_counts, weights, waves, waves, stiffness.reshape(1, -1), legendre)
        anywhere = pl.BlockSpec(memory_space=pl.ANY)
        return pl.pallas_call(
            write_out,
            out_shape=jax.ShapeDtypeStruct(grid.shape, grid.dtype),
            in_specs=[vmem],
            out_specs=anywhere,
            scratch_shapes=[pltpu.SemaphoreType.DMA((pairs,))],
        )(pltpu.with_memory_space_constraint(result, pltpu.VMEM))

    in_specs = (P("lat", None, "lev", None), P("lat"), P(), P("lat", None, None), P("lat"), P())
    out_specs = P("lat", None, "lev", None)
    return jax.shard_map(
        on_device, mesh=mesh, in_specs=in_specs, out_specs=out_specs, check_vma=False
    )
```

```python
import functools
import math

import jax
import jax.numpy as jnp
from jax import lax
from jax.experimental import pallas as pl
from jax.experimental.pallas import tpu as pltpu
from jax.sharding import PartitionSpec as P

MESH = pl.DeviceIdType.MESH
F32 = jnp.float32
BF16 = jnp.bfloat16
LANES = 128
BLOCK = 256
FINE = 16
VMEM_LIMIT = 60 * 2**20
SPLIT = ((0, 8), (8, 16))
OUTWARD = (((0, 6),), ((0, 6),))
HOMEWARD = (((0, 6),), ((0, 2), (2, 2), (4, 2)))
NT = (((1,), (1,)), ((), ()))


def cos_sin(steps, waves, count, inverse):
    product = steps * waves
    turns = jnp.floor(product * inverse + 0.5)
    half = (product - turns * count) * inverse * math.pi
    square = half * half
    sine = half
    term = 1.0
    series_s, series_c = 0.0, 0.0
    for power in range(5, -1, -1):
        series_s = series_s * square + (-1.0) ** power / math.factorial(2 * power + 1)
    for power in range(6, -1, -1):
        series_c = series_c * square + (-1.0) ** power / math.factorial(2 * power)
    sine = half * series_s
    return 1.0 - 2.0 * sine * sine, 2.0 * sine * series_c


def kernel(
    shape,
    grid_ref, counts_ref, weights_ref, waves_smem, wave_row, stiffness_ref, legendre_ref,
    out_ref,
    waves_ref, tables, turn_c, turn_s, small_c, small_s, flat, back, spread, basis, ordered, perm,
    scaled,
    damping, points, operand, turned, send_a, recv_a, send_b, recv_b, basis_sem, send_sems, recv_sems,
):
    holders, pairs, fields, length, slots, width = shape
    blocks = -(-length // BLOCK)
    me = lax.axis_index("lat")
    lev = lax.axis_index("lev")

    barrier = pltpu.get_barrier_semaphore()

    def greet(k, carry):
        other = lax.rem(me + k, holders)
        pl.semaphore_signal(barrier, inc=1, device_id=(other, lev), device_id_type=MESH)
        return carry

    lax.fori_loop(1, holders, greet, 0)
    load_basis = pltpu.make_async_copy(legendre_ref, basis, basis_sem)
    load_basis.start()

    spread[...] = jnp.zeros_like(spread)
    for ref in points:
        ref[...] = jnp.zeros_like(ref)

    for i in range(pairs):
        place = lax.broadcasted_iota(jnp.int32, (holders, width), 0) * pairs + i
        at = lax.broadcasted_iota(jnp.int32, (holders, width), 1)
        perm[i * holders : (i + 1) * holders, :] = jnp.where(at == place, 1.0, 0.0).astype(BF16)
    order = wave_row[...].reshape(1, width)
    first = lax.broadcasted_iota(jnp.int32, (16, width), 0) == 0
    digits = jnp.where(first, order // LANES, lax.rem(order, LANES))
    digits = lax.dot_general(
        digits.astype(F32).astype(BF16), perm[...], NT, preferred_element_type=F32
    )
    waves_ref[...] = digits[:1] * LANES + digits[1:2]

    def build_tables(i):
        count = jnp.full((1, width), counts_ref[i].astype(F32), F32)
        inverse = 1.0 / count
        waves = waves_ref[...]
        steps = lax.broadcasted_iota(jnp.int32, (FINE, width), 0).astype(F32)
        fine_c, fine_s = cos_sin(steps, waves, count, inverse)
        coarse_c, coarse_s = cos_sin(steps * FINE, waves, count, inverse)
        block_c, block_s = cos_sin(steps * BLOCK, waves, count, inverse)
        small_c[...] = coarse_c
        small_s[...] = coarse_s
        turn_c[i] = block_c
        turn_s[i] = block_s
        for g in range(BLOCK // FINE):
            c = small_c[g : g + 1, :]
            s = small_s[g : g + 1, :]
            tables[i, g * FINE : (g + 1) * FINE, :width] = (fine_c * c - fine_s * s).astype(BF16)
            tables[i, g * FINE : (g + 1) * FINE, width:] = (fine_s * c + fine_c * s).astype(BF16)

    def row_of(i, s, count, h, r):
        return pl.multiple_of(((i * slots + s) * 4 + h * 2 + r) * count, 8)

    def analyse(i, chunk):
        start, count = SPLIT[chunk]
        rows = 2 * count
        total = counts_ref[i]
        for t in range(blocks):
            size = min(BLOCK, length - t * BLOCK)
            at = lax.broadcasted_iota(jnp.int32, (rows, size), 1) + t * BLOCK
            values = grid_ref[i, :, start : start + count, t * BLOCK : t * BLOCK + size].astype(F32)
            values = jnp.where(at < total, values.reshape(rows, size), 0.0)
            points[chunk][t * rows : (t + 1) * rows, :size] = values.astype(BF16)
        limit = total.astype(F32)
        scale = jnp.full((1, BLOCK), weights_ref[i], F32) / jnp.full((1, BLOCK), limit, F32)
        for n in range(width // BLOCK):
            lanes = slice(n * BLOCK, (n + 1) * BLOCK)
            by_c = jnp.dot(points[chunk][...], tables[i, :, lanes], preferred_element_type=F32)
            by_s = jnp.dot(
                points[chunk][...],
                tables[i, :, width + n * BLOCK : width + (n + 1) * BLOCK],
                preferred_element_type=F32,
            )
            real = by_c[:rows]
            imag = by_s[:rows]
            for t in range(1, blocks):
                c = turn_c[i, t : t + 1, lanes]
                s = turn_s[i, t : t + 1, lanes]
                zc = by_c[t * rows : (t + 1) * rows]
                zs = by_s[t * rows : (t + 1) * rows]
                real = real + (c * zc - s * zs)
                imag = imag + (s * zc + c * zs)
            inside = 2.0 * waves_ref[:, lanes] < limit
            factor = jnp.where(inside, scale, 0.0)
            real = real * factor
            imag = -imag * factor
            for k in range(BLOCK // LANES):
                slot = n * (BLOCK // LANES) + k
                cut = slice(k * LANES, (k + 1) * LANES)
                for h in range(2):
                    part = slice(h * count, (h + 1) * count)
                    flat[pl.ds(row_of(i, slot, count, h, 0), count), :] = real[part, cut]
                    flat[pl.ds(row_of(i, slot, count, h, 1), count), :] = imag[part, cut]

    def cut_of(chunk, first, number):
        size = slots * 4 * SPLIT[chunk][1]
        return first * size, number * size // LANES

    def pack(source, target, cut):
        deep = 2 * target.shape[1]
        base, pieces = cut
        for q in range(pieces):
            piece = source[base + q * LANES : base + (q + 1) * LANES, :]
            spread[pl.ds(q, holders, stride=deep), :] = piece.T
        twos = spread[pl.ds(0, holders * deep), :].reshape(holders * deep // 2, 2, LANES).astype(BF16)
        target[...] = twos.reshape(holders, deep // 2, 2, LANES)

    def unpack(source, cut):
        deep = 2 * source.shape[1]
        base, pieces = cut
        spread[pl.ds(0, holders * deep), :] = source[...].astype(F32).reshape(holders * deep, LANES)
        for q in range(pieces):
            flat[base + q * LANES : base + (q + 1) * LANES, :] = spread[
                pl.ds(q, holders, stride=deep), :
            ].T

    def send(source, target, sem):
        def one(k, carry):
            other = lax.rem(me + k, holders)
            pltpu.make_async_remote_copy(
                src_ref=source.at[other],
                dst_ref=target.at[me],
                send_sem=send_sems.at[sem],
                recv_sem=recv_sems.at[sem],
                device_id=(other, lev),
                device_id_type=MESH,
            ).start()
            return carry

        lax.fori_loop(1, holders, one, 0)
        target[me] = source[me]

    def finish(ref, sem):
        most = ref.at[pl.ds(0, holders - 1)]
        pltpu.make_async_copy(most, most, sem).wait()

    outward = [(chunk, cut) for chunk, cuts in enumerate(OUTWARD) for cut in cuts]
    homeward = [(chunk, cut) for chunk, cuts in enumerate(HOMEWARD) for cut in cuts]
    for index, (chunk, (first_lat, number)) in enumerate(outward):
        def step(i, carry):
            if chunk == 0:
                build_tables(i)
            analyse(i, chunk)
            return carry

        lax.fori_loop(first_lat, first_lat + number, step, 0)
        pack(flat, send_a[index], cut_of(chunk, first_lat, number))
        if index == 0:
            pl.semaphore_wait(barrier, holders - 1)
        send(send_a[index], recv_a[index], index)

    load_basis.wait()
    levels = lax.broadcasted_iota(jnp.int32, (fields, stiffness_ref.shape[1]), 0) + lev * fields
    column = lax.broadcasted_iota(jnp.int32, (fields, stiffness_ref.shape[1]), 1)
    stiffness = jnp.sum(jnp.where(levels == column, stiffness_ref[...], 0.0), axis=1, keepdims=True)
    offsets = lax.broadcasted_iota(jnp.int32, (1, width), 1)
    parity = (1 - 2 * lax.rem(offsets, 2)).astype(F32)

    def prepare(s, carry):
        for m in range(width // BLOCK):
            part = slice(m * BLOCK, (m + 1) * BLOCK)
            ordered[s, part, :] = jnp.dot(
                perm[part, :], basis[s], preferred_element_type=F32
            ).astype(BF16)
        wave = waves_smem[me * slots + s]
        degrees = (offsets + wave).astype(F32)
        factor = 1.0 / (1.0 + stiffness * degrees * (degrees + 1.0))
        damping[s] = jnp.where(offsets < width - wave, factor, 0.0)
        return carry

    lax.fori_loop(0, slots, prepare, 0)

    for chunk, (start, count) in enumerate(SPLIT):
        for index, (of, cut) in enumerate(outward):
            if of == chunk:
                finish(recv_a[index], recv_sems.at[index])
                unpack(recv_a[index], cut_of(chunk, *cut))

        def project(s, carry):
            parts = [flat[pl.ds(row_of(i, s, count, 0, 0), 4 * count), :].astype(BF16) for i in range(pairs)]
            spectra = jnp.dot(
                jnp.concatenate(parts, axis=1), ordered[s], preferred_element_type=F32
            )
            combined = spectra[: 2 * count] + parity * spectra[2 * count :]
            damp = damping[s, start : start + count, :]
            north = combined * jnp.concatenate([damp, damp], axis=0)
            scaled[s, : 2 * count, :] = north.astype(BF16)
            scaled[s, 2 * count : 4 * count, :] = (north * parity).astype(BF16)
            return carry

        lax.fori_loop(0, slots, project, 0)
        for index, (of, (first_lat, number)) in enumerate(homeward):
            if of != chunk:
                continue

            def restore(s, carry):
                result = lax.dot_general(
                    scaled[s, : 4 * count, :],
                    ordered[s, first_lat * holders : (first_lat + number) * holders, :],
                    NT,
                    preferred_element_type=F32,
                )
                for i in range(number):
                    back[pl.ds(row_of(first_lat + i, s, count, 0, 0), 4 * count), :] = result[
                        :, i * holders : (i + 1) * holders
                    ]
                return carry

            lax.fori_loop(0, slots, restore, 0)
            pack(back, send_b[index], cut_of(chunk, first_lat, number))
            send(send_b[index], recv_b[index], len(outward) + index)

    def synthesise(i, chunk, room):
        start, count = SPLIT[chunk]
        rows = 2 * count
        total = counts_ref[i]
        inside = 2.0 * waves_ref[...] < total.astype(F32)
        weight = jnp.where(inside, jnp.where(waves_ref[...] == 0, 1.0, 2.0), 0.0)
        for s in range(slots):
            lanes = slice(s * LANES, (s + 1) * LANES)
            for h in range(2):
                part = slice(h * count, (h + 1) * count)
                for r in range(2):
                    operand[room, r, part, lanes] = (
                        flat[pl.ds(row_of(i, s, count, h, r), count), :] * weight[:, lanes]
                    )
        for n in range(width // BLOCK):
            lanes = slice(n * BLOCK, (n + 1) * BLOCK)
            real = operand[room, 0, :rows, lanes]
            imag = operand[room, 1, :rows, lanes]
            for t in range(blocks):
                c = turn_c[i, t : t + 1, lanes]
                s = turn_s[i, t : t + 1, lanes]
                turned[room, t * rows : (t + 1) * rows, lanes] = (real * c - imag * s).astype(BF16)
                turned[room, t * rows : (t + 1) * rows, width + n * BLOCK : width + (n + 1) * BLOCK] = (
                    -(real * s + imag * c)
                ).astype(BF16)
        result = lax.dot_general(
            turned[room, : blocks * rows, :], tables[i], NT, preferred_element_type=F32
        )
        for t in range(blocks):
            size = min(BLOCK, length - t * BLOCK)
            at = lax.broadcasted_iota(jnp.int32, (rows, size), 1) + t * BLOCK
            values = jnp.where(at < total, result[t * rows : (t + 1) * rows, :size], 0.0)
            out_ref[i, :, start : start + count, t * BLOCK : t * BLOCK + size] = values.reshape(
                2, count, size
            ).astype(BF16)

    for index, (chunk, (first_lat, number)) in enumerate(homeward):
        finish(recv_b[index], recv_sems.at[len(outward) + index])
        unpack(recv_b[index], cut_of(chunk, first_lat, number))

        def step_back(n, carry):
            synthesise(first_lat + 2 * n, chunk, 0)
            synthesise(first_lat + 2 * n + 1, chunk, 1)
            return carry

        assert number % 2 == 0
        lax.fori_loop(0, number // 2, step_back, 0)

    for index in range(len(outward)):
        finish(send_a[index], send_sems.at[index])
    for index in range(len(homeward)):
        finish(send_b[index], send_sems.at[len(outward) + index])


def write_out(source, target, sems):
    copies = [
        pltpu.make_async_copy(source.at[i], target.at[i], sems.at[i])
        for i in range(source.shape[0])
    ]
    for copy in copies:
        copy.start()
    for copy in copies:
        copy.wait()


def solution(mesh):
    holders = mesh.shape["lat"]

    def on_device(grid, point_counts, waves, legendre, weights, stiffness):
        pairs, _, fields, length = grid.shape
        slots, latitudes, width = legendre.shape
        blocks = -(-length // BLOCK)
        most = max(count for _, count in SPLIT)
        def messages(plan):
            sizes = [
                number * slots * 4 * SPLIT[chunk][1]
                for chunk, cuts in enumerate(plan)
                for _, number in cuts
            ]
            assert all(size % LANES == 0 for size in sizes)
            return [pltpu.VMEM((holders, -(-size // (2 * LANES)), 2, LANES), BF16) for size in sizes]

        outward, homeward = messages(OUTWARD), messages(HOMEWARD)
        deep = 2 * max(message.shape[1] for message in outward + homeward)
        held = pairs * slots * 4 * most
        assert pairs == slots and holders * slots == width == latitudes
        assert sum(count for _, count in SPLIT) == fields
        smem = pl.BlockSpec(memory_space=pltpu.SMEM)
        vmem = pl.BlockSpec(memory_space=pltpu.VMEM)
        result = pl.pallas_call(
            functools.partial(kernel, (holders, pairs, fields, length, slots, width)),
            out_shape=pltpu.VMEM(grid.shape, grid.dtype),
            in_specs=[vmem, smem, smem, smem, vmem, vmem, pl.BlockSpec(memory_space=pl.ANY)],
            out_specs=vmem,
            scratch_shapes=[
                pltpu.VMEM((1, width), F32),
                pltpu.VMEM((pairs, BLOCK, 2 * width), BF16),
                pltpu.VMEM((pairs, FINE, width), F32),
                pltpu.VMEM((pairs, FINE, width), F32),
                pltpu.VMEM((FINE, width), F32),
                pltpu.VMEM((FINE, width), F32),
                pltpu.VMEM((held, LANES), F32),
                pltpu.VMEM((held, LANES), F32),
                pltpu.VMEM((deep * holders, LANES), F32),
                pltpu.VMEM((slots, latitudes, width), BF16),
                pltpu.VMEM((slots, latitudes, width), BF16),
                pltpu.VMEM((latitudes, width), BF16),
                pltpu.VMEM((slots, 4 * most, width), BF16),
                pltpu.VMEM((slots, fields, width), F32),
                [pltpu.VMEM((blocks * 2 * count, BLOCK), BF16) for _, count in SPLIT],
                pltpu.VMEM((2, 2, 2 * most, width), F32),
                pltpu.VMEM((2, blocks * 2 * most, 2 * width), BF16),
                outward,
                outward,
                homeward,
                homeward,
                pltpu.SemaphoreType.DMA,
                pltpu.SemaphoreType.DMA((len(outward) + len(homeward),)),
                pltpu.SemaphoreType.DMA((len(outward) + len(homeward),)),
            ],
            compiler_params=pltpu.CompilerParams(
                collective_id=0, has_side_effects=True, vmem_limit_bytes=VMEM_LIMIT
            ),
        )(grid, point_counts, weights, waves, waves, stiffness.reshape(1, -1), legendre)
        anywhere = pl.BlockSpec(memory_space=pl.ANY)
        return pl.pallas_call(
            write_out,
            out_shape=jax.ShapeDtypeStruct(grid.shape, grid.dtype),
            in_specs=[vmem],
            out_specs=anywhere,
            scratch_shapes=[pltpu.SemaphoreType.DMA((pairs,))],
        )(pltpu.with_memory_space_constraint(result, pltpu.VMEM))

    in_specs = (P("lat", None, "lev", None), P("lat"), P(), P("lat", None, None), P("lat"), P())
    out_specs = P("lat", None, "lev", None)
    return jax.shard_map(
        on_device, mesh=mesh, in_specs=in_specs, out_specs=out_specs, check_vma=False
    )
```
